32 devices in a mesh: groups: 2 (over y), expert: 4 (over z), tensor: 4 (over x, core).
Axes of the slice: x: 2, y: 2, z: 4, core: 2. Of those that a mesh axis runs over, the one named last changes fastest.
Arguments:
- hidden_in: bfloat16 [1536, 3072], P(('groups', 'expert'), 'tensor'), parts along dimension 0, may hold values from -81 to 81
- norm_gain: float32 [3072], P('tensor'), may hold values from 0.1 to 1.9
- router_weight: float32 [3072, 4], P('tensor'), may hold values from -0.109375 to 0.109375
- routes: int32 [1536, 2], P(('groups', 'expert')), parts along dimension 0, may hold values from 0 to 3, all different within a row; in each aligned block of 192 rows (0 to 191, 192 to 383, ...) at most 128 rows name the same one
- gate_weight: bfloat16 [4, 3072, 8192], P('expert', None, 'tensor'), may hold values from -0.109375 to 0.109375
- up_weight: bfloat16 [4, 3072, 8192], P('expert', None, 'tensor'), may hold values from -0.109375 to 0.109375
- down_weight: bfloat16 [4, 8192, 3072], P('expert', 'tensor'), may hold values from -0.0625 to 0.0625
- grad_out: bfloat16 [1536, 3072], P(('groups', 'expert'), 'tensor'), parts along dimension 0, may hold values from -6 to 6
Outputs:
- grad_input: bfloat16 [1536, 3072], P(('groups', 'expert'), 'tensor'), parts along dimension 0
- grad_gain: float32 [6144], P(('groups', 'tensor')), parts along dimension 0
- grad_router: float32 [6144, 4], P(('groups', 'tensor')), parts along dimension 0
- grad_down: bfloat16 [8, 8192, 3072], P(('groups', 'expert'), 'tensor'), parts along dimension 0
The draws below stay inside these ranges and needn't reach their ends.
There are 2 independent parts, one for each index of `groups`. The reference program is written for one: setup_inputs(seed, part) draws one part's arguments, and reference() takes and returns one part's arrays. A program takes and returns all parts, laid end to end along the dimension named above; an argument that names none is the same for every part. Nothing has to cross between parts.
Inputs may be any that keep to these rules, and one draw needn't show every extreme that they name: `routes`: each row names two different experts. Within the rows of one device no expert is named by more than 128 rows, and in every draw some expert is named by exactly 128 rows of some device.
All inputs are finite; a program needn't handle non-finite values.
Results may differ from the reference program's by a relative error of at most 0.0076.
Values may be sent and summed in bfloat16 or wider, within the bound.
A program may use at most 192 MiB of HBM per device.

```python
import math
import jax
import jax.numpy as jnp
import numpy as np
from jax import lax

D = 3072
FF = 8192
TOK_DEV = 192
EXPERTS = 4
TOKENS = 768
CAP = 128
N_EXPERT = 4


def draw_hidden_in(key, part):
    key = jax.random.fold_in(key, 11)
    key_vals, key_rows, key_cols = jax.random.split(key, 3)
    feature_pos = jnp.arange(D, dtype=jnp.float32) / D
    values_raw = jax.random.truncated_normal(key_vals, -3.0, 3.0, (TOKENS, D), jnp.float32)
    rising = jnp.exp(feature_pos * 0.5 * math.log(3.0))
    row_scale = jnp.exp(jax.random.uniform(key_rows, (TOKENS, 1), jnp.float32, math.log(0.3), math.log(3.0)))
    col_scale = jnp.exp(jax.random.uniform(key_cols, (1, D), jnp.float32, math.log(0.3), math.log(3.0)))
    return (values_raw * row_scale * col_scale * rising[None, :]).astype(jnp.bfloat16)


def level_of(rng, shape, cuts, smallest, high):
    level = 1.0
    for axis_at, parts in cuts:
        draws = jax.random.uniform(jax.random.fold_in(jax.random.fold_in(rng, 6), axis_at), (parts,), jnp.float32, smallest / len(cuts), high / len(cuts))
        level = level * jnp.repeat(jnp.exp(draws), shape[axis_at] // parts).reshape((-1,) + (1,) * (len(shape) - 1 - axis_at))
    return level


def deal_out(stream_key, own, number, rows, amount, top, limit, lean):
    sequence = jax.random.permutation(stream_key, amount)
    crowded, ordinary = load_shares(amount, rows * top, limit, lean, True), load_shares(amount, rows * top, limit, lean, False)
    places = jnp.arange(amount)

    def named(tallies, rotation):
        used = int((tallies > 0).sum())
        fixed = max(1, used // 4)
        shifted = fixed + (places - fixed + rotation * (used - fixed)) % max(1, amount - fixed)
        return jnp.zeros((amount,), jnp.int32).at[sequence[jnp.where(places < fixed, places, shifted)]].set(jnp.asarray(tallies, jnp.int32))

    tallies = jnp.where(number % 4 == 0, named(crowded, number // 4), named(ordinary, number - number // 4 - 1))
    mixed = jax.random.permutation(jax.random.fold_in(own, 3), amount)
    giver, sink = mixed[0:amount // 2 * 2:2], mixed[1:amount // 2 * 2:2]
    slack = jnp.minimum(tallies[giver] - 1, limit - tallies[sink]) // 2
    slack = jnp.where((giver == sequence[0]) | (sink == sequence[0]) | (tallies[sink] == 0), 0, jnp.maximum(slack, 0))
    shifted = jax.random.randint(jax.random.fold_in(own, 4), (amount // 2,), 0, 1 << 20) % (slack + 1)
    tallies = tallies.at[giver].add(-shifted).at[sink].add(shifted)
    members = jnp.searchsorted(jnp.cumsum(tallies), jnp.arange(rows * top), side="right").astype(jnp.int32)
    table = members.reshape(top, rows).T
    table = table[jax.random.permutation(jax.random.fold_in(own, 1), rows)]
    rotation = jax.random.randint(jax.random.fold_in(own, 2), (rows, 1), 0, top)
    return jnp.take_along_axis(table, (jnp.arange(top)[None, :] + rotation) % top, axis=1)


def load_shares(amount, total, reach, slope, full):
    weights = [(1 << 20) // math.isqrt(standing ** slope) + 1 for standing in range(1, amount + 1)]
    largest = reach if full else min(reach, max(-(-total // amount), total * weights[0] // sum(weights)))
    least = 1 if total - largest >= amount - 1 else 0
    counts, surplus = [largest] + [least] * (amount - 1), total - largest - least * (amount - 1)
    while surplus > 0:
        free = [i for i in range(1, amount) if counts[i] < largest] or [i for i in range(1, amount) if counts[i] < reach]
        mass, budget = sum([weights[i] for i in free]), surplus
        for i in free:
            addition = min(reach - counts[i], max(1, budget * weights[i] // mass), surplus)
            counts[i] = counts[i] + addition
            surplus = surplus - addition
    return np.array(counts)


def noise(rng, shape, deviation, limit, cuts=(), kind=jnp.bfloat16):
    values = jax.random.normal(rng, shape, jnp.float32) * deviation
    if len(cuts) > 0:
        values = level_of(rng, shape, cuts, -0.22, 0.18) * values
    return jnp.clip(values, min=-limit, max=limit).astype(kind)


def setup_inputs(seed: int = 0, part: int = 0) -> dict:
    key_of = jax.random.split(jax.random.key(seed), 9)
    part_splits = jax.random.split(jax.random.fold_in(key_of[8], part), 9)
    hidden_in = draw_hidden_in(jax.random.fold_in(jax.random.fold_in(key_of[8], part), 71), part)
    norm_gain = jnp.clip(1.0 + 0.18 * jax.random.normal(key_of[1], (D,), jnp.float32), 0.1, 1.9)
    router_weight = noise(key_of[2], (D, EXPERTS), D ** -0.5, 0.109375, ((0, 4),), jnp.float32)
    routes_keys = jax.random.split(jax.random.fold_in(part_splits[3], 1), TOKENS // TOK_DEV)
    routes_turns = jax.random.permutation(jax.random.fold_in(part_splits[3], 3), TOKENS // TOK_DEV)
    routes = jax.vmap(lambda own, number: deal_out(jax.random.fold_in(part_splits[3], 2), own, number, TOK_DEV, EXPERTS, 2, CAP, 2))(routes_keys, routes_turns).reshape((TOKENS, 2))
    gate_weight = noise(key_of[4], (EXPERTS, D, FF), D ** -0.5, 0.109375, ((0, 4), (2, 4)))
    up_weight = noise(key_of[5], (EXPERTS, D, FF), D ** -0.5, 0.109375, ((0, 4), (2, 4)))
    down_weight = noise(key_of[6], (EXPERTS, FF, D), FF ** -0.5, 0.0625, ((0, 4), (1, 4)))
    grad_out = noise(part_splits[7], (TOKENS, D), 1.0, 6.0, ((0, 4), (1, 4)))
    return dict(hidden_in=hidden_in, norm_gain=norm_gain, router_weight=router_weight, routes=routes, gate_weight=gate_weight, up_weight=up_weight, down_weight=down_weight, grad_out=grad_out)


EPS = 1e-05
PRECISE = lax.Precision.HIGHEST

def expert_pass(packed):
    slot_rows, slot_grads, slot_prob, gate_matrix, up_matrix, down_matrix = packed
    gate_pre = jnp.dot(slot_rows, gate_matrix, preferred_element_type=jnp.float32)
    up_pre = jnp.dot(slot_rows, up_matrix, preferred_element_type=jnp.float32)
    gate_sig = jax.nn.sigmoid(gate_pre)
    hidden_act = (gate_pre * gate_sig * up_pre).astype(jnp.bfloat16)
    expert_out = jnp.dot(hidden_act, down_matrix, preferred_element_type=jnp.float32)
    prob_grad = lax.optimization_barrier(jnp.sum(slot_grads.astype(jnp.float32) * expert_out, axis=1))
    out_grad = (slot_prob.astype(jnp.float32)[:, None] * slot_grads.astype(jnp.float32)).astype(jnp.bfloat16)
    down_grad = jnp.einsum('sf,sd->fd', hidden_act, out_grad, preferred_element_type=jnp.float32).astype(jnp.bfloat16)
    act_grad = jnp.einsum('sd,fd->sf', out_grad, down_matrix, preferred_element_type=jnp.float32)
    gate_grad = (act_grad * up_pre * gate_sig * (1.0 + gate_pre * (1.0 - gate_sig))).astype(jnp.bfloat16)
    up_grad = (act_grad * gate_pre * gate_sig).astype(jnp.bfloat16)
    row_grad = jnp.einsum('sf,df->sd', gate_grad, gate_matrix, preferred_element_type=jnp.float32)
    row_grad = row_grad + jnp.einsum('sf,df->sd', up_grad, up_matrix, preferred_element_type=jnp.float32)
    inner = lax.optimization_barrier(jnp.sum(slot_rows.astype(jnp.float32) * row_grad, axis=1))
    return (row_grad, inner, prob_grad, down_grad)

def reference(hidden_in, norm_gain, router_weight, routes, gate_weight, up_weight, down_weight, grad_out):
    inputs_f = hidden_in.astype(jnp.float32)
    mean_square = lax.optimization_barrier(jnp.mean(inputs_f * inputs_f, axis=1, keepdims=True))
    inv_rms = lax.rsqrt(mean_square + EPS)
    normed = inputs_f * inv_rms * norm_gain[None, :]
    normed_b = normed.astype(jnp.bfloat16)
    logits = jnp.dot(normed, router_weight, precision=PRECISE)
    labels = jnp.arange(EXPERTS, dtype=jnp.int32)
    first_hot = (routes[:, 0:1] == labels[None, :]).astype(jnp.float32)
    second_hot = (routes[:, 1:2] == labels[None, :]).astype(jnp.float32)
    prob_first = jax.nn.sigmoid(lax.optimization_barrier(jnp.sum(logits * (first_hot - second_hot), axis=1)))
    prob_second = 1.0 - prob_first
    prob_b = jnp.stack([prob_first, prob_second], axis=1).astype(jnp.bfloat16)
    slot_count = N_EXPERT * CAP
    flat_routes = routes.reshape(-1)
    route_hot = (flat_routes[:, None] == labels[None, :]).astype(jnp.int32)
    slot_rank = lax.optimization_barrier(jnp.sum((jnp.cumsum(route_hot, axis=0, dtype=jnp.int32) - route_hot) * route_hot, axis=1, dtype=jnp.int32))
    slot_index = (flat_routes * slot_count + slot_rank).astype(jnp.int32)
    source_row = jnp.repeat(jnp.arange(TOKENS, dtype=jnp.int32), 2)
    row_buffer = jnp.zeros((EXPERTS * slot_count, D), jnp.bfloat16).at[slot_index].set(normed_b[source_row])
    grad_buffer = jnp.zeros((EXPERTS * slot_count, D), jnp.bfloat16).at[slot_index].set(grad_out[source_row])
    prob_buffer = jnp.zeros((EXPERTS * slot_count,), jnp.bfloat16).at[slot_index].set(prob_b.reshape(-1))
    row_grads, inners, prob_grads, grad_down = lax.map(expert_pass, (row_buffer.reshape(EXPERTS, slot_count, D), grad_buffer.reshape(EXPERTS, slot_count, D), prob_buffer.reshape(EXPERTS, slot_count), gate_weight, up_weight, down_weight))
    back_rows = row_grads.reshape(EXPERTS * slot_count, D)[slot_index].reshape(TOKENS, 2, D)
    back_inner = inners.reshape(-1)[slot_index].reshape(TOKENS, 2)
    back_prob = prob_grads.reshape(-1)[slot_index].reshape(TOKENS, 2)
    gap_grad = (back_prob[:, 0] - back_prob[:, 1]) * prob_first * prob_second
    logit_grad = gap_grad[:, None] * (first_hot - second_hot)
    total_grad = back_rows[:, 0] + back_rows[:, 1] + jnp.dot(logit_grad, router_weight.T, precision=PRECISE)
    norm_dot = (back_inner[:, 0] + back_inner[:, 1] + lax.optimization_barrier(jnp.sum(logits * logit_grad, axis=1))) / inv_rms[:, 0]
    cubed = inv_rms * inv_rms * inv_rms
    grad_input = (inv_rms * norm_gain[None, :] * total_grad - inputs_f * cubed * (norm_dot[:, None] / D)).astype(jnp.bfloat16)
    grad_gain = lax.optimization_barrier(jnp.sum(total_grad * inputs_f * inv_rms, axis=0))
    grad_router = jnp.dot(normed.T, logit_grad, precision=PRECISE)
    return (grad_input, grad_gain, grad_router, grad_down)
```

```python
import jax
import jax.numpy as jnp
from jax import lax
from jax.sharding import PartitionSpec as P

EPS = 1e-05
PRECISE = lax.Precision.HIGHEST


def body(
    hidden_in, norm_gain, router_weight, routes, gate_weight, up_weight, down_weight, grad_out
):
    tok_rows, part_cols = hidden_in.shape
    expert_count = router_weight.shape[1]
    feat_width = part_cols * lax.axis_size("tensor")
    capacity = 8 * tok_rows // (3 * expert_count)
    inputs_f = hidden_in.astype(jnp.float32)
    scaled_in = inputs_f * norm_gain[None, :]
    square_part = jnp.sum(inputs_f * inputs_f, axis=1)
    logit_part = jnp.dot(scaled_in, router_weight, precision=PRECISE)
    square_sum, logit_sum = lax.psum((square_part, logit_part), "tensor")
    inv_rms = lax.rsqrt(square_sum / feat_width + EPS)[:, None]
    normed = scaled_in * inv_rms
    normed_b = normed.astype(jnp.bfloat16)
    logits = logit_sum * inv_rms
    labels = jnp.arange(expert_count, dtype=jnp.int32)
    first_hot = (routes[:, 0:1] == labels[None, :]).astype(jnp.float32)
    second_hot = (routes[:, 1:2] == labels[None, :]).astype(jnp.float32)
    prob_first = jax.nn.sigmoid(jnp.sum(logits * (first_hot - second_hot), axis=1))
    prob_second = 1.0 - prob_first
    flat_routes = routes.reshape(-1)
    route_hot = (flat_routes[:, None] == labels[None, :]).astype(jnp.int32)
    slot_rank = jnp.sum(
        (jnp.cumsum(route_hot, axis=0, dtype=jnp.int32) - route_hot) * route_hot,
        axis=1,
        dtype=jnp.int32,
    )
    slot_index = (flat_routes * capacity + slot_rank).reshape(tok_rows, 2)
    slot_ids = jnp.arange(expert_count * capacity, dtype=jnp.int32)
    pick_first = (slot_index[:, 0:1] == slot_ids[None, :]).astype(jnp.float32)
    pick_second = (slot_index[:, 1:2] == slot_ids[None, :]).astype(jnp.float32)
    pick_both = pick_first + pick_second
    pick_bf = pick_both.astype(jnp.bfloat16)
    prob_first_b = prob_first.astype(jnp.bfloat16)
    prob_second_b = prob_second.astype(jnp.bfloat16)
    pick_weight = (
        pick_first * prob_first_b.astype(jnp.float32)[:, None]
        + pick_second * prob_second_b.astype(jnp.float32)[:, None]
    ).astype(jnp.bfloat16)

    def dispatch(pick, row_block):
        placed = jnp.einsum("ts,td->sd", pick, row_block, preferred_element_type=jnp.float32)
        return placed.astype(jnp.bfloat16).reshape(expert_count, capacity, row_block.shape[1])

    send_grads = dispatch(pick_weight, grad_out)
    send_rows = dispatch(pick_bf, normed_b)
    got_rows = lax.all_to_all(send_rows, "expert", split_axis=0, concat_axis=0, tiled=True)
    got_grads = lax.all_to_all(send_grads, "expert", split_axis=0, concat_axis=0, tiled=True)
    slot_total = got_rows.shape[0] * capacity
    slot_rows = lax.all_gather(got_rows, "tensor", axis=2, tiled=True)
    slot_rows = slot_rows.reshape(slot_total, feat_width)
    out_grad = lax.all_gather(got_grads, "tensor", axis=2, tiled=True)
    out_grad = out_grad.reshape(slot_total, feat_width)
    gate_matrix = gate_weight[0]
    up_matrix = up_weight[0]
    down_matrix = down_weight[0]
    gate_pre = jnp.dot(slot_rows, gate_matrix, preferred_element_type=jnp.float32)
    up_pre = jnp.dot(slot_rows, up_matrix, preferred_element_type=jnp.float32)
    gate_sig = jax.nn.sigmoid(gate_pre)
    hidden_act = (gate_pre * gate_sig * up_pre).astype(jnp.bfloat16)
    grad_down = jnp.einsum(
        "sf,sd->fd", hidden_act, out_grad, preferred_element_type=jnp.float32
    ).astype(jnp.bfloat16)[None]
    act_grad = jnp.einsum("sd,fd->sf", out_grad, down_matrix, preferred_element_type=jnp.float32)
    gate_grad = (act_grad * up_pre * gate_sig * (1.0 + gate_pre * (1.0 - gate_sig))).astype(
        jnp.bfloat16
    )
    up_grad = (act_grad * gate_pre * gate_sig).astype(jnp.bfloat16)
    row_part = jnp.einsum("sf,df->sd", gate_grad, gate_matrix, preferred_element_type=jnp.float32)
    row_part = row_part + jnp.einsum(
        "sf,df->sd", up_grad, up_matrix, preferred_element_type=jnp.float32
    )
    prob_part = jnp.sum(hidden_act.astype(jnp.float32) * act_grad, axis=1)
    inner_part = jnp.sum(
        gate_grad.astype(jnp.float32) * gate_pre + up_grad.astype(jnp.float32) * up_pre, axis=1
    )
    row_own = lax.psum_scatter(
        row_part.astype(jnp.bfloat16), "tensor", scatter_dimension=1, tiled=True
    )
    back_rows = lax.all_to_all(
        row_own.reshape(-1, capacity, part_cols), "expert", split_axis=0, concat_axis=0, tiled=True
    ).reshape(expert_count * capacity, part_cols)
    scalars = jnp.stack([inner_part, prob_part], axis=0).reshape(2, -1, capacity)
    scalars = lax.all_to_all(scalars, "expert", split_axis=1, concat_axis=1, tiled=True)
    scalars = scalars.reshape(2, expert_count * capacity)
    pick_token = jnp.concatenate([pick_first, pick_second], axis=0)
    token_scalars = jnp.einsum("cs,ts->ct", scalars, pick_token, precision=PRECISE)
    token_scalars = lax.psum(token_scalars, "tensor").reshape(2, 2, tok_rows)
    expert_grad = jnp.dot(pick_bf, back_rows, preferred_element_type=jnp.float32)
    token_inner = token_scalars[0, 0] + token_scalars[0, 1]
    ratio_first = prob_first / jnp.where(prob_first_b == 0, 1, prob_first_b).astype(jnp.float32)
    ratio_second = prob_second / jnp.where(prob_second_b == 0, 1, prob_second_b).astype(jnp.float32)
    gap_grad = (
        token_scalars[1, 0] * ratio_first * prob_second
        - token_scalars[1, 1] * ratio_second * prob_first
    )
    logit_grad = gap_grad[:, None] * (first_hot - second_hot)
    total_grad = expert_grad + jnp.einsum("te,de->td", logit_grad, router_weight, precision=PRECISE)
    norm_dot = (token_inner + jnp.sum(logits * logit_grad, axis=1)) / inv_rms[:, 0]
    cubed = inv_rms * inv_rms * inv_rms
    grad_input = (
        inv_rms * norm_gain[None, :] * total_grad
        - inputs_f * cubed * (norm_dot[:, None] / feat_width)
    ).astype(jnp.bfloat16)
    gain_part = jnp.sum(total_grad * inputs_f * inv_rms, axis=0)
    router_part = jnp.einsum("td,te->de", normed, logit_grad, precision=PRECISE)
    sums = lax.psum(jnp.concatenate([gain_part[None, :], router_part.T], axis=0), "expert")
    grad_gain, grad_router = sums[0], sums[1:].T
    return (grad_input, grad_gain, grad_router, grad_down)


def solution(mesh):
    placed = (
        P(("groups", "expert"), "tensor"),
        P("tensor"),
        P("tensor", None),
        P(("groups", "expert"), None),
        P("expert", None, "tensor"),
        P("expert", None, "tensor"),
        P("expert", "tensor", None),
        P(("groups", "expert"), "tensor"),
    )
    return jax.shard_map(
        body,
        mesh=mesh,
        in_specs=placed,
        out_specs=(
            P(("groups", "expert"), "tensor"),
            P(("groups", "tensor")),
            P(("groups", "tensor"), None),
            P(("groups", "expert"), "tensor", None),
        ),
        check_vma=False,
    )
```

```python
import jax
import jax.numpy as jnp
from jax import lax
from jax.experimental import pallas as pl
from jax.experimental.pallas import tpu as pltpu
from jax.sharding import PartitionSpec as P

EPS = 1e-05
PRECISE = lax.Precision.HIGHEST


def meet(peers):
    barrier = pltpu.get_barrier_semaphore()
    for peer in peers:
        pl.semaphore_signal(barrier, inc=1, device_id=peer, device_id_type=pl.DeviceIdType.MESH)
    pl.semaphore_wait(barrier, len(peers))


def remote(src, dst, send, recv, peer):
    return pltpu.make_async_remote_copy(
        src_ref=src,
        dst_ref=dst,
        send_sem=send,
        recv_sem=recv,
        device_id=peer,
        device_id_type=pl.DeviceIdType.MESH,
    )


def small_psum(part, axis, collective_id):
    count = lax.axis_size(axis)

    def kernel(part_ref, out_ref, land, send, recv):
        me = lax.axis_index(axis)
        peers = [{axis: lax.rem(me + k, count)} for k in range(1, count)]
        meet(peers)
        copies = [
            remote(part_ref, land.at[me], send.at[k], recv.at[k], peer)
            for k, peer in enumerate(peers)
        ]
        for copy in copies:
            copy.start()
        land[me] = part_ref[...]
        for copy in copies:
            copy.wait_recv()
        total = land[0]
        for source in range(1, count):
            total = total + land[source]
        out_ref[...] = total
        for copy in copies:
            copy.wait_send()

    return pl.pallas_call(
        kernel,
        out_shape=jax.ShapeDtypeStruct(part.shape, part.dtype),
        in_specs=[pl.BlockSpec(memory_space=pltpu.VMEM)],
        out_specs=pl.BlockSpec(memory_space=pltpu.VMEM),
        scratch_shapes=[
            pltpu.VMEM((count,) + part.shape, part.dtype),
            pltpu.SemaphoreType.DMA((count - 1,)),
            pltpu.SemaphoreType.DMA((count - 1,)),
        ],
        compiler_params=pltpu.CompilerParams(collective_id=collective_id, has_side_effects=True),
    )(part)


def gather_slots(send_grads, send_rows):
    experts, capacity, cols = send_rows.shape
    slots = experts * capacity

    def kernel(
        grads_ref, rows_ref, out_grads, out_rows,
        own_sem, z_send, z_recv, x_send, x_recv, m_send, m_recv, n_send, n_recv,
    ):
        z = lax.axis_index("expert")
        t = lax.axis_index("tensor")
        over_x = {"tensor": lax.rem(t + 2, 4)}
        mate = {"tensor": t + 1 - 2 * lax.rem(t, 2)}
        zs = [lax.rem(z + k, experts) for k in range(experts)]
        from_z = [lax.rem(z + experts - k, experts) for k in range(experts)]
        outs = (out_grads, out_rows)
        ins = (grads_ref, rows_ref)
        meet([over_x, mate] + [{"expert": zd} for zd in zs[1:]])

        def block(a, source, quarter):
            return outs[a].at[
                pl.ds(pl.multiple_of(source * capacity, capacity), capacity),
                pl.ds(pl.multiple_of(quarter * cols, 128), cols),
            ]

        z_copies = {}
        for a in range(2):
            for k in (2, 3, 1)[: experts - 1]:
                copy = remote(
                    ins[a].at[zs[k]], block(a, z, t), z_send.at[a, k], z_recv.at[a, k],
                    {"expert": zs[k]},
                )
                copy.start()
                z_copies[a, k] = copy
        x_copies, m_copies, n_copies = {}, {}, {}
        quarter_x = lax.rem(t + 2, 4)
        order = [(a, k) for a in range(2) for k in (0, 1, 3, 2)]

        def pass_on(a, k):
            far = block(a, from_z[k], quarter_x)
            x_copies[a, k].wait_recv()
            n_copies[a, k] = remote(far, far, n_send.at[a, k], n_recv.at[a, k], mate)
            n_copies[a, k].start()

        for i, (a, k) in enumerate(order):
            near = block(a, from_z[k], t)
            if k == 0:
                own = pltpu.make_async_copy(ins[a].at[z], near, own_sem.at[a])
                own.start()
                own.wait()
            else:
                z_copies[a, k].wait_recv()
            x_copies[a, k] = remote(near, near, x_send.at[a, k], x_recv.at[a, k], over_x)
            x_copies[a, k].start()
            m_copies[a, k] = remote(near, near, m_send.at[a, k], m_recv.at[a, k], mate)
            m_copies[a, k].start()
            if i:
                pass_on(*order[i - 1])
        pass_on(*order[-1])
        for group in (m_copies, n_copies):
            for copy in group.values():
                copy.wait_recv()
        for group in (z_copies, x_copies, m_copies, n_copies):
            for copy in group.values():
                copy.wait_send()

    sems = [pltpu.SemaphoreType.DMA((2, experts)) for _ in range(8)]
    shape = jax.ShapeDtypeStruct((slots, 4 * cols), send_rows.dtype)
    return pl.pallas_call(
        kernel,
        out_shape=(shape, shape),
        in_specs=[pl.BlockSpec(memory_space=pltpu.VMEM)] * 2,
        out_specs=[pl.BlockSpec(memory_space=pltpu.VMEM)] * 2,
        scratch_shapes=[pltpu.SemaphoreType.DMA((2,))] + sems,
        compiler_params=pltpu.CompilerParams(
            collective_id=2, has_side_effects=True, vmem_limit_bytes=24 * 1024 * 1024
        ),
    )(send_grads, send_rows)


def return_slots(row_part, scalars, experts, capacity, cols):
    def kernel(
        part_ref, scal_ref, out_rows, out_scal,
        m_land, x_out, kept, x_land, z_out, s_land, s_x, s_xland, s_z,
        m_send, m_recv, x_send, x_recv, z_send, z_recv,
        sm_send, sm_recv, sx_send, sx_recv, sz_send, sz_recv,
    ):
        z = lax.axis_index("expert")
        t = lax.axis_index("tensor")
        x_mine = t // 2
        core = lax.rem(t, 2)
        over_x = {"tensor": lax.rem(t + 2, 4)}
        mate = {"tensor": t + 1 - 2 * core}
        zs = [lax.rem(z + k, experts) for k in range(experts)]
        order = (2, 3, 1, 0)
        meet([over_x, mate] + [{"expert": zd} for zd in zs[1:]])

        def rows(k):
            return pl.ds(pl.multiple_of(zs[k] * capacity, capacity), capacity)

        def lanes(quarter):
            return pl.ds(pl.multiple_of(quarter * cols, 128), cols)

        pending = []
        s_m = remote(scal_ref, s_land, sm_send, sm_recv, mate)
        m_copies = {}
        for n, k in enumerate(order):
            for j in range(2):
                xq = lax.rem(x_mine + 1 + j, 2)
                m_copies[k, j] = remote(
                    part_ref.at[rows(k), lanes(2 * xq + 1 - core)],
                    m_land.at[k, j], m_send.at[k, j], m_recv.at[k, j], mate,
                )
                m_copies[k, j].start()
            if n == 0:
                s_m.start()
        pending += list(m_copies.values()) + [s_m]
        x_copies, z_copies = {}, {}
        quarter_x = lax.rem(t + 2, 4)

        def finish(k):
            x_copies[k].wait_recv()
            z_out[k] = (kept[k] + x_land[k].astype(jnp.float32)).astype(jnp.bfloat16)
            if k:
                z_copies[k] = remote(
                    z_out.at[k], out_rows.at[z], z_send.at[k], z_recv.at[k], {"expert": zs[k]}
                )
                z_copies[k].start()
            else:
                out_rows[z] = z_out[0]

        for n, k in enumerate(order):
            m_copies[k, 0].wait_recv()
            x_out[k] = (
                part_ref[rows(k), lanes(quarter_x)].astype(jnp.float32)
                + m_land[k, 0].astype(jnp.float32)
            ).astype(jnp.bfloat16)
            x_copies[k] = remote(x_out.at[k], x_land.at[k], x_send.at[k], x_recv.at[k], over_x)
            x_copies[k].start()
            if n == 0:
                s_m.wait_recv()
                s_x[...] = scal_ref[...] + s_land[...]
                s_xc = remote(s_x, s_xland, sx_send, sx_recv, over_x)
                s_xc.start()
                pending.append(s_xc)
            m_copies[k, 1].wait_recv()
            kept[k] = part_ref[rows(k), lanes(t)].astype(jnp.float32) + m_land[k, 1].astype(
                jnp.float32
            )
            if n:
                finish(order[n - 1])
            if n == 1:
                s_xc.wait_recv()
                s_z[...] = s_x[...] + s_xland[...]
                for j in range(1, experts):
                    copy = remote(
                        s_z.at[zs[j]], out_scal.at[z], sz_send.at[j], sz_recv.at[j],
                        {"expert": zs[j]},
                    )
                    copy.start()
                    z_copies["s", j] = copy
                out_scal[z] = s_z[z]
        finish(order[-1])
        for copy in z_copies.values():
            copy.wait_recv()
        for copy in pending + list(x_copies.values()) + list(z_copies.values()):
            copy.wait_send()

    f32, bf16, dma = jnp.float32, jnp.bfloat16, pltpu.SemaphoreType.DMA
    chunk = (experts, capacity, cols)
    return pl.pallas_call(
        kernel,
        out_shape=(
            jax.ShapeDtypeStruct(chunk, bf16),
            jax.ShapeDtypeStruct(scalars.shape, f32),
        ),
        in_specs=[pl.BlockSpec(memory_space=pltpu.VMEM)] * 2,
        out_specs=[pl.BlockSpec(memory_space=pltpu.VMEM)] * 2,
        scratch_shapes=[
            pltpu.VMEM((experts, 2, capacity, cols), bf16),
            pltpu.VMEM(chunk, bf16),
            pltpu.VMEM(chunk, f32),
            pltpu.VMEM(chunk, bf16),
            pltpu.VMEM(chunk, bf16),
            pltpu.VMEM(scalars.shape, f32),
            pltpu.VMEM(scalars.shape, f32),
            pltpu.VMEM(scalars.shape, f32),
            pltpu.VMEM(scalars.shape, f32),
            dma((experts, 2)), dma((experts, 2)),
            dma((experts,)), dma((experts,)),
            dma((experts,)), dma((experts,)),
            dma, dma, dma, dma,
            dma((experts,)), dma((experts,)),
        ],
        compiler_params=pltpu.CompilerParams(
            collective_id=3, has_side_effects=True, vmem_limit_bytes=32 * 1024 * 1024
        ),
    )(row_part, scalars)


def body(
    hidden_in, norm_gain, router_weight, routes, gate_weight, up_weight, down_weight, grad_out
):
    tok_rows, part_cols = hidden_in.shape
    expert_count = router_weight.shape[1]
    feat_width = part_cols * lax.axis_size("tensor")
    capacity = 8 * tok_rows // (3 * expert_count)
    direct = lax.axis_size("tensor") == 4 and expert_count == 4 and part_cols % 128 == 0
    inputs_f = hidden_in.astype(jnp.float32)
    scaled_in = inputs_f * norm_gain[None, :]
    square_part = jnp.sum(inputs_f * inputs_f, axis=1)
    logit_part = jnp.einsum("td,de->et", scaled_in, router_weight, precision=PRECISE)
    token_part = jnp.concatenate([square_part[None, :], logit_part], axis=0)
    if direct:
        padding = ((0, -token_part.shape[0] % 8), (0, -tok_rows % 128))
        token_sum = small_psum(jnp.pad(token_part, padding), "tensor", 0)
    else:
        token_sum = lax.psum(token_part, "tensor")
    square_sum = token_sum[0, :tok_rows]
    logit_sum = token_sum[1 : 1 + expert_count, :tok_rows].T
    inv_rms = lax.rsqrt(square_sum / feat_width + EPS)[:, None]
    normed = scaled_in * inv_rms
    normed_b = normed.astype(jnp.bfloat16)
    logits = logit_sum * inv_rms
    labels = jnp.arange(expert_count, dtype=jnp.int32)
    first_hot = (routes[:, 0:1] == labels[None, :]).astype(jnp.float32)
    second_hot = (routes[:, 1:2] == labels[None, :]).astype(jnp.float32)
    prob_first = jax.nn.sigmoid(jnp.sum(logits * (first_hot - second_hot), axis=1))
    prob_second = 1.0 - prob_first
    flat_routes = routes.reshape(-1)
    route_hot = (flat_routes[:, None] == labels[None, :]).astype(jnp.int32)
    slot_rank = jnp.sum(
        (jnp.cumsum(route_hot, axis=0, dtype=jnp.int32) - route_hot) * route_hot,
        axis=1,
        dtype=jnp.int32,
    )
    slot_index = (flat_routes * capacity + slot_rank).reshape(tok_rows, 2)
    slot_ids = jnp.arange(expert_count * capacity, dtype=jnp.int32)
    pick_first = (slot_index[:, 0:1] == slot_ids[None, :]).astype(jnp.float32)
    pick_second = (slot_index[:, 1:2] == slot_ids[None, :]).astype(jnp.float32)
    pick_both = pick_first + pick_second
    pick_bf = pick_both.astype(jnp.bfloat16)
    prob_first_b = prob_first.astype(jnp.bfloat16)
    prob_second_b = prob_second.astype(jnp.bfloat16)
    pick_weight = (
        pick_first * prob_first_b.astype(jnp.float32)[:, None]
        + pick_second * prob_second_b.astype(jnp.float32)[:, None]
    ).astype(jnp.bfloat16)

    def dispatch(pick, row_block):
        placed = jnp.einsum("ts,td->sd", pick, row_block, preferred_element_type=jnp.float32)
        return placed.astype(jnp.bfloat16).reshape(expert_count, capacity, row_block.shape[1])

    send_grads = dispatch(pick_weight, grad_out)
    send_rows = dispatch(pick_bf, normed_b)
    slot_total = expert_count * capacity
    if direct:
        out_grad, slot_rows = gather_slots(send_grads, send_rows)
    else:
        got_rows = lax.all_to_all(send_rows, "expert", split_axis=0, concat_axis=0, tiled=True)
        got_grads = lax.all_to_all(send_grads, "expert", split_axis=0, concat_axis=0, tiled=True)
        slot_rows = lax.all_gather(got_rows, "tensor", axis=2, tiled=True)
        slot_rows = slot_rows.reshape(slot_total, feat_width)
        out_grad = lax.all_gather(got_grads, "tensor", axis=2, tiled=True)
        out_grad = out_grad.reshape(slot_total, feat_width)
    gate_matrix = gate_weight[0]
    up_matrix = up_weight[0]
    down_matrix = down_weight[0]
    gate_pre = jnp.dot(slot_rows, gate_matrix, preferred_element_type=jnp.float32)
    up_pre = jnp.dot(slot_rows, up_matrix, preferred_element_type=jnp.float32)
    gate_sig = jax.nn.sigmoid(gate_pre)
    hidden_act = (gate_pre * gate_sig * up_pre).astype(jnp.bfloat16)
    grad_down = jnp.einsum(
        "sf,sd->fd", hidden_act, out_grad, preferred_element_type=jnp.float32
    ).astype(jnp.bfloat16)[None]
    act_grad = jnp.einsum("sd,fd->sf", out_grad, down_matrix, preferred_element_type=jnp.float32)
    gate_grad = (act_grad * up_pre * gate_sig * (1.0 + gate_pre * (1.0 - gate_sig))).astype(
        jnp.bfloat16
    )
    up_grad = (act_grad * gate_pre * gate_sig).astype(jnp.bfloat16)
    row_part = jnp.einsum("sf,df->sd", gate_grad, gate_matrix, preferred_element_type=jnp.float32)
    row_part = row_part + jnp.einsum(
        "sf,df->sd", up_grad, up_matrix, preferred_element_type=jnp.float32
    )
    prob_part = jnp.sum(hidden_act.astype(jnp.float32) * act_grad, axis=1)
    inner_part = jnp.sum(
        gate_grad.astype(jnp.float32) * gate_pre + up_grad.astype(jnp.float32) * up_pre, axis=1
    )
    row_part = row_part.astype(jnp.bfloat16)
    if direct:
        scalars = jnp.stack([inner_part, prob_part], axis=0).reshape(2, expert_count, capacity)
        scalars = jnp.pad(scalars.transpose(1, 0, 2), ((0, 0), (0, 6), (0, 0)))
        back_rows, scalars = return_slots(row_part, scalars, expert_count, capacity, part_cols)
        back_rows = back_rows.reshape(slot_total, part_cols)
        scalars = scalars[:, :2].transpose(1, 0, 2).reshape(2, slot_total)
    else:
        row_own = lax.psum_scatter(
            row_part, "tensor", scatter_dimension=1, tiled=True
        )
        back_rows = lax.all_to_all(
            row_own.reshape(-1, capacity, part_cols), "expert", split_axis=0, concat_axis=0, tiled=True
        ).reshape(expert_count * capacity, part_cols)
        scalars = jnp.stack([inner_part, prob_part], axis=0).reshape(2, -1, capacity)
        scalars = lax.all_to_all(scalars, "expert", split_axis=1, concat_axis=1, tiled=True)
        scalars = scalars.reshape(2, expert_count * capacity)
    pick_token = jnp.concatenate([pick_first, pick_second], axis=0)
    token_scalars = jnp.einsum("cs,ts->ct", scalars, pick_token, precision=PRECISE)
    if not direct:
        token_scalars = lax.psum(token_scalars, "tensor")
    token_scalars = token_scalars.reshape(2, 2, tok_rows)
    expert_grad = jnp.dot(pick_bf, back_rows, preferred_element_type=jnp.float32)
    token_inner = token_scalars[0, 0] + token_scalars[0, 1]
    ratio_first = prob_first / jnp.where(prob_first_b == 0, 1, prob_first_b).astype(jnp.float32)
    ratio_second = prob_second / jnp.where(prob_second_b == 0, 1, prob_second_b).astype(jnp.float32)
    gap_grad = (
        token_scalars[1, 0] * ratio_first * prob_second
        - token_scalars[1, 1] * ratio_second * prob_first
    )
    logit_grad = gap_grad[:, None] * (first_hot - second_hot)
    total_grad = expert_grad + jnp.einsum("te,de->td", logit_grad, router_weight, precision=PRECISE)
    norm_dot = (token_inner + jnp.sum(logits * logit_grad, axis=1)) / inv_rms[:, 0]
    cubed = inv_rms * inv_rms * inv_rms
    grad_input = (
        inv_rms * norm_gain[None, :] * total_grad
        - inputs_f * cubed * (norm_dot[:, None] / feat_width)
    ).astype(jnp.bfloat16)
    gain_part = jnp.sum(total_grad * inputs_f * inv_rms, axis=0)
    router_part = jnp.einsum("td,te->de", normed, logit_grad, precision=PRECISE)
    sums = jnp.concatenate([gain_part[None, :], router_part.T], axis=0)
    if direct:
        sums = small_psum(jnp.pad(sums, ((0, -sums.shape[0] % 8), (0, 0))), "expert", 1)
        sums = sums[: 1 + expert_count]
    else:
        sums = lax.psum(sums, "expert")
    grad_gain, grad_router = sums[0], sums[1:].T
    return (grad_input, grad_gain, grad_router, grad_down)


def solution(mesh):
    placed = (
        P(("groups", "expert"), "tensor"),
        P("tensor"),
        P("tensor", None),
        P(("groups", "expert"), None),
        P("expert", None, "tensor"),
        P("expert", None, "tensor"),
        P("expert", "tensor", None),
        P(("groups", "expert"), "tensor"),
    )
    return jax.shard_map(
        body,
        mesh=mesh,
        in_specs=placed,
        out_specs=(
            P(("groups", "expert"), "tensor"),
            P(("groups", "tensor")),
            P(("groups", "tensor"), None),
            P(("groups", "expert"), "tensor", None),
        ),
        check_vma=False,
    )
```

```python
import jax
import jax.numpy as jnp
from jax import lax
from jax.experimental import pallas as pl
from jax.experimental.pallas import tpu as pltpu
from jax.sharding import PartitionSpec as P

EPS = 1e-05
PRECISE = lax.Precision.HIGHEST


def meet(peers):
    barrier = pltpu.get_barrier_semaphore()
    for peer in peers:
        pl.semaphore_signal(barrier, inc=1, device_id=peer, device_id_type=pl.DeviceIdType.MESH)
    pl.semaphore_wait(barrier, len(peers))


def remote(src, dst, send, recv, peer):
    return pltpu.make_async_remote_copy(
        src_ref=src,
        dst_ref=dst,
        send_sem=send,
        recv_sem=recv,
        device_id=peer,
        device_id_type=pl.DeviceIdType.MESH,
    )


def small_psum(part, axis, collective_id):
    count = lax.axis_size(axis)

    def kernel(part_ref, out_ref, land, send, recv):
        me = lax.axis_index(axis)
        peers = [{axis: lax.rem(me + k, count)} for k in range(1, count)]
        meet(peers)
        copies = [
            remote(part_ref, land.at[me], send.at[k], recv.at[k], peer)
            for k, peer in enumerate(peers)
        ]
        for copy in copies:
            copy.start()
        land[me] = part_ref[...]
        for copy in copies:
            copy.wait_recv()
        total = land[0]
        for source in range(1, count):
            total = total + land[source]
        out_ref[...] = total
        for copy in copies:
            copy.wait_send()

    return pl.pallas_call(
        kernel,
        out_shape=jax.ShapeDtypeStruct(part.shape, part.dtype),
        in_specs=[pl.BlockSpec(memory_space=pltpu.VMEM)],
        out_specs=pl.BlockSpec(memory_space=pltpu.VMEM),
        scratch_shapes=[
            pltpu.VMEM((count,) + part.shape, part.dtype),
            pltpu.SemaphoreType.DMA((count - 1,)),
            pltpu.SemaphoreType.DMA((count - 1,)),
        ],
        compiler_params=pltpu.CompilerParams(collective_id=collective_id, has_side_effects=True),
    )(part)


TRANSPOSED = (((1,), (1,)), ((), ()))
STRIP = 256


def gather_slots(send_grads, send_rows, down_matrix):
    experts, capacity, cols = send_rows.shape
    slots = experts * capacity
    hidden = down_matrix.shape[0]
    strips = hidden // STRIP

    def kernel(
        grads_ref, rows_ref, down_ref, out_grads, out_rows, out_act,
        down_held, down_sem, own_sem, z_send, z_recv, x_send, x_recv, m_send, m_recv, n_send, n_recv,
    ):
        z = lax.axis_index("expert")
        t = lax.axis_index("tensor")
        over_x = {"tensor": lax.rem(t + 2, 4)}
        mate = {"tensor": t + 1 - 2 * lax.rem(t, 2)}
        zs = [lax.rem(z + k, experts) for k in range(experts)]
        from_z = [lax.rem(z + experts - k, experts) for k in range(experts)]
        outs = (out_grads, out_rows)
        ins = (grads_ref, rows_ref)
        meet([over_x, mate] + [{"expert": zd} for zd in zs[1:]])

        def block(a, source, quarter):
            return outs[a].at[
                pl.ds(pl.multiple_of(source * capacity, capacity), capacity),
                pl.ds(pl.multiple_of(quarter * cols, 128), cols),
            ]

        load_down = pltpu.make_async_copy(down_ref, down_held, down_sem)
        load_down.start()
        z_copies, x_copies, m_copies, n_copies = {}, {}, {}, {}
        quarter_x = lax.rem(t + 2, 4)
        sequence = (0, 1, 3, 2)

        def send_z(a, k):
            z_copies[a, k] = remote(
                ins[a].at[zs[k]], block(a, z, t), z_send.at[a, k], z_recv.at[a, k],
                {"expert": zs[k]},
            )
            z_copies[a, k].start()

        def forward(a, k):
            near = block(a, from_z[k], t)
            if k == 0:
                own = pltpu.make_async_copy(ins[a].at[z], near, own_sem.at[a])
                own.start()
                own.wait()
            else:
                z_copies[a, k].wait_recv()
                if a == 0:
                    send_z(1, k)
            x_copies[a, k] = remote(near, near, x_send.at[a, k], x_recv.at[a, k], over_x)
            x_copies[a, k].start()
            m_copies[a, k] = remote(near, near, m_send.at[a, k], m_recv.at[a, k], mate)
            m_copies[a, k].start()

        def pass_on(a, k):
            far = block(a, from_z[k], quarter_x)
            x_copies[a, k].wait_recv()
            n_copies[a, k] = remote(far, far, n_send.at[a, k], n_recv.at[a, k], mate)
            n_copies[a, k].start()

        def multiply(first, last):
            @pl.loop(first, last)
            def _(strip):
                span = pl.ds(pl.multiple_of(strip * STRIP, STRIP), STRIP)
                out_act[:, span] = lax.dot_general(
                    out_grads[...], down_held[span, :], TRANSPOSED,
                    preferred_element_type=jnp.float32,
                )

        for k in sequence[1:]:
            send_z(0, k)
        for i, k in enumerate(sequence):
            forward(0, k)
            if i:
                pass_on(0, sequence[i - 1])
        forward(1, 0)
        pass_on(0, sequence[-1])
        for k in range(experts):
            m_copies[0, k].wait_recv()
            n_copies[0, k].wait_recv()
        load_down.wait()
        for i, k in enumerate(sequence[1:]):
            forward(1, k)
            pass_on(1, sequence[i])
            multiply(strips * i // 4, strips * (i + 1) // 4)
        pass_on(1, sequence[-1])
        multiply(strips * 3 // 4, strips)
        for k in range(experts):
            m_copies[1, k].wait_recv()
            n_copies[1, k].wait_recv()
        for group in (z_copies, x_copies, m_copies, n_copies):
            for copy in group.values():
                copy.wait_send()

    sems = [pltpu.SemaphoreType.DMA((2, experts)) for _ in range(8)]
    shape = jax.ShapeDtypeStruct((slots, 4 * cols), send_rows.dtype)
    vmem = pl.BlockSpec(memory_space=pltpu.VMEM)
    return pl.pallas_call(
        kernel,
        out_shape=(shape, shape, jax.ShapeDtypeStruct((slots, hidden), jnp.float32)),
        in_specs=[vmem, vmem, pl.BlockSpec(memory_space=pl.ANY)],
        out_specs=[vmem] * 3,
        scratch_shapes=[
            pltpu.VMEM(down_matrix.shape, down_matrix.dtype),
            pltpu.SemaphoreType.DMA,
            pltpu.SemaphoreType.DMA((2,)),
        ]
        + sems,
        compiler_params=pltpu.CompilerParams(
            collective_id=2, has_side_effects=True, vmem_limit_bytes=50 * 1024 * 1024
        ),
    )(send_grads, send_rows, down_matrix)


def return_slots(gate_grad, up_grad, gate_matrix, up_matrix, scalars, experts, capacity, cols):
    width = gate_grad.shape[1]
    half = 2 * capacity

    def kernel(
        gg_ref, ug_ref, gate_ref, up_ref, scal_ref, out_rows, out_scal,
        lhs, held, part, m_out, m_land, x_out, x_land, z_out, s_land, s_x, s_xland, s_z,
        w_sem, m_send, m_recv, x_send, x_recv, z_send, z_recv,
        sm_send, sm_recv, sx_send, sx_recv, sz_send, sz_recv,
    ):
        z = lax.axis_index("expert")
        t = lax.axis_index("tensor")
        core = lax.rem(t, 2)
        t_x = lax.rem(t + 2, 4)
        t_mate = t + 1 - 2 * core
        over_x, mate = {"tensor": t_x}, {"tensor": t_mate}
        zs = [lax.rem(z + k, experts) for k in range(experts)]
        order = (2, 3, 1, 0)
        quarters = (lax.rem(t_mate + 2, 4), t_x, t_mate, t)
        loads = []
        for n, quarter in enumerate(quarters):
            span = pl.ds(pl.multiple_of(quarter * cols, cols), cols)
            pair = [
                pltpu.make_async_copy(ref.at[span, :], held.at[i, n], w_sem.at[i, n])
                for i, ref in enumerate((gate_ref, up_ref))
            ]
            for load in pair:
                load.start()
            loads.append(pair)
        meet([over_x, mate] + [{"expert": zd} for zd in zs[1:]])
        s_m = remote(scal_ref, s_land, sm_send, sm_recv, mate)
        s_m.start()
        for n, k in enumerate(order):
            rows = pl.ds(pl.multiple_of(zs[k] * capacity, capacity), capacity)
            lhs[0, n * capacity : (n + 1) * capacity, :] = gg_ref[rows, :]
            lhs[1, n * capacity : (n + 1) * capacity, :] = ug_ref[rows, :]

        def multiply(h, n):
            if h == 0:
                for load in loads[n]:
                    load.wait()

            @pl.loop(0, cols // STRIP)
            def _(strip):
                span = pl.ds(pl.multiple_of(strip * STRIP, STRIP), STRIP)
                total = 0.0
                for i in range(2):
                    total = total + lax.dot_general(
                        lhs[i, h * half : (h + 1) * half, :], held[i, n, span, :], TRANSPOSED,
                        preferred_element_type=jnp.float32,
                    )
                if n in (0, 2):
                    m_out[h, n // 2, :, span] = total.astype(jnp.bfloat16)
                else:
                    part[h, n // 2, :, span] = total

        m_copies, x_copies, z_copies, s_copies = {}, {}, {}, []

        def send_mate(h, j):
            m_copies[h, j] = remote(
                m_out.at[h, j], m_land.at[h, j], m_send.at[h, j], m_recv.at[h, j], mate
            )
            m_copies[h, j].start()

        def finish(h):
            m_copies[h, 1].wait_recv()
            x_copies[h].wait_recv()
            total = part[h, 1] + m_land[h, 1].astype(jnp.float32) + x_land[h].astype(jnp.float32)
            z_out[h] = total.astype(jnp.bfloat16)
            for i in range(2):
                k = order[2 * h + i]
                block = z_out.at[h, i * capacity : (i + 1) * capacity, :]
                if k:
                    z_copies[k] = remote(
                        block, out_rows.at[z], z_send.at[k], z_recv.at[k], {"expert": zs[k]}
                    )
                    z_copies[k].start()
                else:
                    out_rows[z] = z_out[h, i * capacity : (i + 1) * capacity, :]

        for h in range(2):
            multiply(h, 0)
            send_mate(h, 0)
            if h == 1:
                finish(0)
            multiply(h, 1)
            m_copies[h, 0].wait_recv()
            x_out[h] = (part[h, 0] + m_land[h, 0].astype(jnp.float32)).astype(jnp.bfloat16)
            x_copies[h] = remote(
                x_out.at[h], x_land.at[h], x_send.at[h], x_recv.at[h], over_x
            )
            x_copies[h].start()
            if h == 0:
                s_m.wait_recv()
                s_x[...] = scal_ref[...] + s_land[...]
                s_xc = remote(s_x, s_xland, sx_send, sx_recv, over_x)
                s_xc.start()
            multiply(h, 2)
            send_mate(h, 1)
            if h == 0:
                s_xc.wait_recv()
                s_z[...] = s_x[...] + s_xland[...]
                for j in range(1, experts):
                    copy = remote(
                        s_z.at[zs[j]], out_scal.at[z], sz_send.at[j], sz_recv.at[j],
                        {"expert": zs[j]},
                    )
                    copy.start()
                    s_copies.append(copy)
                out_scal[z] = s_z[z]
            multiply(h, 3)
        finish(1)
        for copy in list(z_copies.values()) + s_copies:
            copy.wait_recv()
        for copy in list(m_copies.values()) + list(x_copies.values()) + [s_m, s_xc]:
            copy.wait_send()
        for copy in list(z_copies.values()) + s_copies:
            copy.wait_send()

    f32, bf16, dma = jnp.float32, jnp.bfloat16, pltpu.SemaphoreType.DMA
    vmem = pl.BlockSpec(memory_space=pltpu.VMEM)
    anywhere = pl.BlockSpec(memory_space=pl.ANY)
    return pl.pallas_call(
        kernel,
        out_shape=(
            jax.ShapeDtypeStruct((experts, capacity, cols), bf16),
            jax.ShapeDtypeStruct(scalars.shape, f32),
        ),
        in_specs=[vmem, vmem, anywhere, anywhere, vmem],
        out_specs=[vmem] * 2,
        scratch_shapes=[
            pltpu.VMEM((2, 2 * half, width), bf16),
            pltpu.VMEM((2, 4, cols, width), bf16),
            pltpu.VMEM((2, 2, half, cols), f32),
            pltpu.VMEM((2, 2, half, cols), bf16),
            pltpu.VMEM((2, 2, half, cols), bf16),
            pltpu.VMEM((2, half, cols), bf16),
            pltpu.VMEM((2, half, cols), bf16),
            pltpu.VMEM((2, half, cols), bf16),
            pltpu.VMEM(scalars.shape, f32),
            pltpu.VMEM(scalars.shape, f32),
            pltpu.VMEM(scalars.shape, f32),
            pltpu.VMEM(scalars.shape, f32),
            dma((2, 4)),
            dma((2, 2)), dma((2, 2)),
            dma((2,)), dma((2,)),
            dma((experts,)), dma((experts,)),
            dma, dma, dma, dma,
            dma((experts,)), dma((experts,)),
        ],
        compiler_params=pltpu.CompilerParams(
            collective_id=3, has_side_effects=True, vmem_limit_bytes=58 * 1024 * 1024
        ),
    )(gate_grad, up_grad, gate_matrix, up_matrix, scalars)


def body(
    hidden_in, norm_gain, router_weight, routes, gate_weight, up_weight, down_weight, grad_out
):
    tok_rows, part_cols = hidden_in.shape
    expert_count = router_weight.shape[1]
    feat_width = part_cols * lax.axis_size("tensor")
    capacity = 8 * tok_rows // (3 * expert_count)
    direct = lax.axis_size("tensor") == 4 and expert_count == 4 and part_cols % STRIP == 0 and down_weight.shape[1] % STRIP == 0
    inputs_f = hidden_in.astype(jnp.float32)
    scaled_in = inputs_f * norm_gain[None, :]
    square_part = jnp.sum(inputs_f * inputs_f, axis=1)
    logit_part = jnp.einsum("td,de->et", scaled_in, router_weight, precision=PRECISE)
    token_part = jnp.concatenate([square_part[None, :], logit_part], axis=0)
    if direct:
        padding = ((0, -token_part.shape[0] % 8), (0, -tok_rows % 128))
        token_sum = small_psum(jnp.pad(token_part, padding), "tensor", 0)
    else:
        token_sum = lax.psum(token_part, "tensor")
    square_sum = token_sum[0, :tok_rows]
    logit_sum = token_sum[1 : 1 + expert_count, :tok_rows].T
    inv_rms = lax.rsqrt(square_sum / feat_width + EPS)[:, None]
    normed = scaled_in * inv_rms
    normed_b = normed.astype(jnp.bfloat16)
    logits = logit_sum * inv_rms
    labels = jnp.arange(expert_count, dtype=jnp.int32)
    first_hot = (routes[:, 0:1] == labels[None, :]).astype(jnp.float32)
    second_hot = (routes[:, 1:2] == labels[None, :]).astype(jnp.float32)
    prob_first = jax.nn.sigmoid(jnp.sum(logits * (first_hot - second_hot), axis=1))
    prob_second = 1.0 - prob_first
    flat_routes = routes.reshape(-1)
    route_hot = (flat_routes[:, None] == labels[None, :]).astype(jnp.int32)
    slot_rank = jnp.sum(
        (jnp.cumsum(route_hot, axis=0, dtype=jnp.int32) - route_hot) * route_hot,
        axis=1,
        dtype=jnp.int32,
    )
    slot_index = (flat_routes * capacity + slot_rank).reshape(tok_rows, 2)
    slot_ids = jnp.arange(expert_count * capacity, dtype=jnp.int32)
    pick_first = (slot_index[:, 0:1] == slot_ids[None, :]).astype(jnp.float32)
    pick_second = (slot_index[:, 1:2] == slot_ids[None, :]).astype(jnp.float32)
    pick_both = pick_first + pick_second
    pick_bf = pick_both.astype(jnp.bfloat16)
    prob_first_b = prob_first.astype(jnp.bfloat16)
    prob_second_b = prob_second.astype(jnp.bfloat16)
    pick_weight = (
        pick_first * prob_first_b.astype(jnp.float32)[:, None]
        + pick_second * prob_second_b.astype(jnp.float32)[:, None]
    ).astype(jnp.bfloat16)

    def dispatch(pick, row_block):
        placed = jnp.einsum("ts,td->sd", pick, row_block, preferred_element_type=jnp.float32)
        return placed.astype(jnp.bfloat16).reshape(expert_count, capacity, row_block.shape[1])

    send_grads = dispatch(pick_weight, grad_out)
    send_rows = dispatch(pick_bf, normed_b)
    slot_total = expert_count * capacity
    if direct:
        out_grad, slot_rows, act_grad = gather_slots(send_grads, send_rows, down_weight[0])
    else:
        got_rows = lax.all_to_all(send_rows, "expert", split_axis=0, concat_axis=0, tiled=True)
        got_grads = lax.all_to_all(send_grads, "expert", split_axis=0, concat_axis=0, tiled=True)
        slot_rows = lax.all_gather(got_rows, "tensor", axis=2, tiled=True)
        slot_rows = slot_rows.reshape(slot_total, feat_width)
        out_grad = lax.all_gather(got_grads, "tensor", axis=2, tiled=True)
        out_grad = out_grad.reshape(slot_total, feat_width)
    gate_matrix = gate_weight[0]
    up_matrix = up_weight[0]
    down_matrix = down_weight[0]
    gate_pre = jnp.dot(slot_rows, gate_matrix, preferred_element_type=jnp.float32)
    up_pre = jnp.dot(slot_rows, up_matrix, preferred_element_type=jnp.float32)
    gate_sig = jax.nn.sigmoid(gate_pre)
    hidden_act = (gate_pre * gate_sig * up_pre).astype(jnp.bfloat16)
    grad_down = jnp.einsum(
        "sf,sd->fd", hidden_act, out_grad, preferred_element_type=jnp.float32
    ).astype(jnp.bfloat16)[None]
    if not direct:
        act_grad = jnp.einsum("sd,fd->sf", out_grad, down_matrix, preferred_element_type=jnp.float32)
    gate_grad = (act_grad * up_pre * gate_sig * (1.0 + gate_pre * (1.0 - gate_sig))).astype(
        jnp.bfloat16
    )
    up_grad = (act_grad * gate_pre * gate_sig).astype(jnp.bfloat16)
    prob_part = jnp.sum(hidden_act.astype(jnp.float32) * act_grad, axis=1)
    inner_part = jnp.sum(
        gate_grad.astype(jnp.float32) * gate_pre + up_grad.astype(jnp.float32) * up_pre, axis=1
    )
    if direct:
        scalars = jnp.stack([inner_part, prob_part], axis=0).reshape(2, expert_count, capacity)
        scalars = jnp.pad(scalars.transpose(1, 0, 2), ((0, 0), (0, 6), (0, 0)))
        back_rows, scalars = return_slots(
            gate_grad, up_grad, gate_matrix, up_matrix, scalars, expert_count, capacity, part_cols
        )
        back_rows = back_rows.reshape(slot_total, part_cols)
        scalars = scalars[:, :2].transpose(1, 0, 2).reshape(2, slot_total)
    else:
        row_part = jnp.einsum("sf,df->sd", gate_grad, gate_matrix, preferred_element_type=jnp.float32)
        row_part = row_part + jnp.einsum(
            "sf,df->sd", up_grad, up_matrix, preferred_element_type=jnp.float32
        )
        row_part = row_part.astype(jnp.bfloat16)
        row_own = lax.psum_scatter(
            row_part, "tensor", scatter_dimension=1, tiled=True
        )
        back_rows = lax.all_to_all(
            row_own.reshape(-1, capacity, part_cols), "expert", split_axis=0, concat_axis=0, tiled=True
        ).reshape(expert_count * capacity, part_cols)
        scalars = jnp.stack([inner_part, prob_part], axis=0).reshape(2, -1, capacity)
        scalars = lax.all_to_all(scalars, "expert", split_axis=1, concat_axis=1, tiled=True)
        scalars = scalars.reshape(2, expert_count * capacity)
    pick_token = jnp.concatenate([pick_first, pick_second], axis=0)
    token_scalars = jnp.einsum("cs,ts->ct", scalars, pick_token, precision=PRECISE)
    if not direct:
        token_scalars = lax.psum(token_scalars, "tensor")
    token_scalars = token_scalars.reshape(2, 2, tok_rows)
    expert_grad = jnp.dot(pick_bf, back_rows, preferred_element_type=jnp.float32)
    token_inner = token_scalars[0, 0] + token_scalars[0, 1]
    ratio_first = prob_first / jnp.where(prob_first_b == 0, 1, prob_first_b).astype(jnp.float32)
    ratio_second = prob_second / jnp.where(prob_second_b == 0, 1, prob_second_b).astype(jnp.float32)
    gap_grad = (
        token_scalars[1, 0] * ratio_first * prob_second
        - token_scalars[1, 1] * ratio_second * prob_first
    )
    logit_grad = gap_grad[:, None] * (first_hot - second_hot)
    total_grad = expert_grad + jnp.einsum("te,de->td", logit_grad, router_weight, precision=PRECISE)
    norm_dot = (token_inner + jnp.sum(logits * logit_grad, axis=1)) / inv_rms[:, 0]
    cubed = inv_rms * inv_rms * inv_rms
    grad_input = (
        inv_rms * norm_gain[None, :] * total_grad
        - inputs_f * cubed * (norm_dot[:, None] / feat_width)
    ).astype(jnp.bfloat16)
    gain_part = jnp.sum(total_grad * inputs_f * inv_rms, axis=0)
    router_part = jnp.einsum("td,te->de", normed, logit_grad, precision=PRECISE)
    sums = jnp.concatenate([gain_part[None, :], router_part.T], axis=0)
    if direct:
        sums = small_psum(jnp.pad(sums, ((0, -sums.shape[0] % 8), (0, 0))), "expert", 1)
        sums = sums[: 1 + expert_count]
    else:
        sums = lax.psum(sums, "expert")
    grad_gain, grad_router = sums[0], sums[1:].T
    return (grad_input, grad_gain, grad_router, grad_down)


def solution(mesh):
    placed = (
        P(("groups", "expert"), "tensor"),
        P("tensor"),
        P("tensor", None),
        P(("groups", "expert"), None),
        P("expert", None, "tensor"),
        P("expert", None, "tensor"),
        P("expert", "tensor", None),
        P(("groups", "expert"), "tensor"),
    )
    return jax.shard_map(
        body,
        mesh=mesh,
        in_specs=placed,
        out_specs=(
            P(("groups", "expert"), "tensor"),
            P(("groups", "tensor")),
            P(("groups", "tensor"), None),
            P(("groups", "expert"), "tensor", None),
        ),
        check_vma=False,
    )
```

```python
import jax
import jax.numpy as jnp
from jax import lax
from jax.experimental import pallas as pl
from jax.experimental.pallas import tpu as pltpu
from jax.sharding import PartitionSpec as P

EPS = 1e-05
PRECISE = lax.Precision.HIGHEST


def meet(peers):
    barrier = pltpu.get_barrier_semaphore()
    for peer in peers:
        pl.semaphore_signal(barrier, inc=1, device_id=peer, device_id_type=pl.DeviceIdType.MESH)
    pl.semaphore_wait(barrier, len(peers))


def remote(src, dst, send, recv, peer):
    return pltpu.make_async_remote_copy(
        src_ref=src,
        dst_ref=dst,
        send_sem=send,
        recv_sem=recv,
        device_id=peer,
        device_id_type=pl.DeviceIdType.MESH,
    )


def small_psum(part, axis, collective_id):
    count = lax.axis_size(axis)

    def kernel(part_ref, out_ref, land, send, recv):
        me = lax.axis_index(axis)
        peers = [{axis: lax.rem(me + k, count)} for k in range(1, count)]
        meet(peers)
        copies = [
            remote(part_ref, land.at[me], send.at[k], recv.at[k], peer)
            for k, peer in enumerate(peers)
        ]
        for copy in copies:
            copy.start()
        land[me] = part_ref[...]
        for copy in copies:
            copy.wait_recv()
        total = land[0]
        for source in range(1, count):
            total = total + land[source]
        out_ref[...] = total
        for copy in copies:
            copy.wait_send()

    return pl.pallas_call(
        kernel,
        out_shape=jax.ShapeDtypeStruct(part.shape, part.dtype),
        in_specs=[pl.BlockSpec(memory_space=pltpu.VMEM)],
        out_specs=pl.BlockSpec(memory_space=pltpu.VMEM),
        scratch_shapes=[
            pltpu.VMEM((count,) + part.shape, part.dtype),
            pltpu.SemaphoreType.DMA((count - 1,)),
            pltpu.SemaphoreType.DMA((count - 1,)),
        ],
        compiler_params=pltpu.CompilerParams(collective_id=collective_id, has_side_effects=True),
    )(part)


TRANSPOSED = (((1,), (1,)), ((), ()))
STRIP = 256


def gather_slots(send_grads, send_rows, down_matrix, gate_matrix):
    experts, capacity, cols = send_rows.shape
    slots = experts * capacity
    hidden = down_matrix.shape[0]
    strips = hidden // STRIP

    def kernel(
        grads_ref, rows_ref, down_ref, gate_ref, out_grads, out_rows, out_act, out_gate,
        down_held, gate_held, lhs, down_sem, gate_sem, own_sem, z_send, z_recv, x_send, x_recv, m_send, m_recv, n_send, n_recv,
    ):
        z = lax.axis_index("expert")
        t = lax.axis_index("tensor")
        over_x = {"tensor": lax.rem(t + 2, 4)}
        mate = {"tensor": t + 1 - 2 * lax.rem(t, 2)}
        zs = [lax.rem(z + k, experts) for k in range(experts)]
        from_z = [lax.rem(z + experts - k, experts) for k in range(experts)]
        outs = (out_grads, out_rows)
        ins = (grads_ref, rows_ref)
        meet([over_x, mate] + [{"expert": zd} for zd in zs[1:]])

        def block(a, source, quarter):
            return outs[a].at[
                pl.ds(pl.multiple_of(source * capacity, capacity), capacity),
                pl.ds(pl.multiple_of(quarter * cols, 128), cols),
            ]

        load_down = pltpu.make_async_copy(down_ref, down_held, down_sem)
        load_down.start()
        load_gate = pltpu.make_async_copy(gate_ref, gate_held, gate_sem)
        load_gate.start()
        z_copies, x_copies, m_copies, n_copies = {}, {}, {}, {}
        quarter_x = lax.rem(t + 2, 4)
        sequence = (0, 1, 3, 2)

        def send_z(a, k):
            z_copies[a, k] = remote(
                ins[a].at[zs[k]], block(a, z, t), z_send.at[a, k], z_recv.at[a, k],
                {"expert": zs[k]},
            )
            z_copies[a, k].start()

        def forward(a, k):
            near = block(a, from_z[k], t)
            if k == 0:
                own = pltpu.make_async_copy(ins[a].at[z], near, own_sem.at[a])
                own.start()
                own.wait()
            else:
                z_copies[a, k].wait_recv()
                if a == 0:
                    send_z(1, k)
            x_copies[a, k] = remote(near, near, x_send.at[a, k], x_recv.at[a, k], over_x)
            x_copies[a, k].start()
            m_copies[a, k] = remote(near, near, m_send.at[a, k], m_recv.at[a, k], mate)
            m_copies[a, k].start()

        def pass_on(a, k):
            far = block(a, from_z[k], quarter_x)
            x_copies[a, k].wait_recv()
            n_copies[a, k] = remote(far, far, n_send.at[a, k], n_recv.at[a, k], mate)
            n_copies[a, k].start()

        def multiply(first, last):
            @pl.loop(first, last)
            def _(strip):
                span = pl.ds(pl.multiple_of(strip * STRIP, STRIP), STRIP)
                out_act[:, span] = lax.dot_general(
                    out_grads[...], down_held[span, :], TRANSPOSED,
                    preferred_element_type=jnp.float32,
                )

        def project(pair):
            for i, k in enumerate(pair):
                m_copies[1, k].wait_recv()
                n_copies[1, k].wait_recv()
                lhs[i * capacity : (i + 1) * capacity, :] = out_rows[source_rows(k), :]

            @pl.loop(0, strips)
            def _(strip):
                span = pl.ds(pl.multiple_of(strip * STRIP, STRIP), STRIP)
                total = jnp.dot(lhs[...], gate_held[:, span], preferred_element_type=jnp.float32)
                for i, k in enumerate(pair):
                    out_gate[source_rows(k), span] = total[i * capacity : (i + 1) * capacity]

        def source_rows(k):
            return pl.ds(pl.multiple_of(from_z[k] * capacity, capacity), capacity)

        for k in sequence[1:]:
            send_z(0, k)
        for i, k in enumerate(sequence):
            forward(0, k)
            if i:
                pass_on(0, sequence[i - 1])
        forward(1, 0)
        pass_on(0, sequence[-1])
        for k in range(experts):
            m_copies[0, k].wait_recv()
            n_copies[0, k].wait_recv()
        load_down.wait()
        for i, k in enumerate(sequence[1:]):
            forward(1, k)
            pass_on(1, sequence[i])
            if i < 2:
                multiply(strips * i // 2, strips * (i + 1) // 2)
        load_gate.wait()
        project(sequence[:2])
        pass_on(1, sequence[-1])
        project(sequence[2:])
        for group in (z_copies, x_copies, m_copies, n_copies):
            for copy in group.values():
                copy.wait_send()

    sems = [pltpu.SemaphoreType.DMA((2, experts)) for _ in range(8)]
    shape = jax.ShapeDtypeStruct((slots, 4 * cols), send_rows.dtype)
    vmem = pl.BlockSpec(memory_space=pltpu.VMEM)
    return pl.pallas_call(
        kernel,
        out_shape=(shape, shape) + (jax.ShapeDtypeStruct((slots, hidden), jnp.float32),) * 2,
        in_specs=[vmem, vmem] + [pl.BlockSpec(memory_space=pl.ANY)] * 2,
        out_specs=[vmem] * 4,
        scratch_shapes=[
            pltpu.VMEM(down_matrix.shape, down_matrix.dtype),
            pltpu.VMEM(gate_matrix.shape, gate_matrix.dtype),
            pltpu.VMEM((2 * capacity, 4 * cols), send_rows.dtype),
            pltpu.SemaphoreType.DMA,
            pltpu.SemaphoreType.DMA,
            pltpu.SemaphoreType.DMA((2,)),
        ]
        + sems,
        compiler_params=pltpu.CompilerParams(
            collective_id=2, has_side_effects=True, vmem_limit_bytes=58 * 1024 * 1024
        ),
    )(send_grads, send_rows, down_matrix, gate_matrix)


def return_slots(gate_grad, up_grad, gate_matrix, up_matrix, scalars, experts, capacity, cols):
    width = gate_grad.shape[1]
    half = 2 * capacity

    def kernel(
        gg_ref, ug_ref, gate_ref, up_ref, scal_ref, out_rows, out_scal,
        lhs, held, part, m_out, m_land, x_out, x_land, z_out, s_land, s_x, s_xland, s_z,
        w_sem, m_send, m_recv, x_send, x_recv, z_send, z_recv,
        sm_send, sm_recv, sx_send, sx_recv, sz_send, sz_recv,
    ):
        z = lax.axis_index("expert")
        t = lax.axis_index("tensor")
        core = lax.rem(t, 2)
        t_x = lax.rem(t + 2, 4)
        t_mate = t + 1 - 2 * core
        over_x, mate = {"tensor": t_x}, {"tensor": t_mate}
        zs = [lax.rem(z + k, experts) for k in range(experts)]
        order = (2, 3, 1, 0)
        quarters = (lax.rem(t_mate + 2, 4), t_x, t_mate, t)
        loads = []
        for n, quarter in enumerate(quarters):
            span = pl.ds(pl.multiple_of(quarter * cols, cols), cols)
            pair = [
                pltpu.make_async_copy(ref.at[span, :], held.at[i, n], w_sem.at[i, n])
                for i, ref in enumerate((gate_ref, up_ref))
            ]
            for load in pair:
                load.start()
            loads.append(pair)
        meet([over_x, mate] + [{"expert": zd} for zd in zs[1:]])
        s_m = remote(scal_ref, s_land, sm_send, sm_recv, mate)
        s_m.start()
        for n, k in enumerate(order):
            rows = pl.ds(pl.multiple_of(zs[k] * capacity, capacity), capacity)
            lhs[0, n * capacity : (n + 1) * capacity, :] = gg_ref[rows, :]
            lhs[1, n * capacity : (n + 1) * capacity, :] = ug_ref[rows, :]

        def multiply(h, n):
            if h == 0:
                for load in loads[n]:
                    load.wait()

            @pl.loop(0, cols // STRIP)
            def _(strip):
                span = pl.ds(pl.multiple_of(strip * STRIP, STRIP), STRIP)
                total = 0.0
                for i in range(2):
                    total = total + lax.dot_general(
                        lhs[i, h * half : (h + 1) * half, :], held[i, n, span, :], TRANSPOSED,
                        preferred_element_type=jnp.float32,
                    )
                if n in (0, 2):
                    m_out[h, n // 2, :, span] = total.astype(jnp.bfloat16)
                else:
                    part[h, n // 2, :, span] = total

        m_copies, x_copies, z_copies, s_copies = {}, {}, {}, []

        def send_mate(h, j):
            m_copies[h, j] = remote(
                m_out.at[h, j], m_land.at[h, j], m_send.at[h, j], m_recv.at[h, j], mate
            )
            m_copies[h, j].start()

        def finish(h):
            m_copies[h, 1].wait_recv()
            x_copies[h].wait_recv()
            total = part[h, 1] + m_land[h, 1].astype(jnp.float32) + x_land[h].astype(jnp.float32)
            z_out[h] = total.astype(jnp.bfloat16)
            for i in range(2):
                k = order[2 * h + i]
                block = z_out.at[h, i * capacity : (i + 1) * capacity, :]
                if k:
                    z_copies[k] = remote(
                        block, out_rows.at[z], z_send.at[k], z_recv.at[k], {"expert": zs[k]}
                    )
                    z_copies[k].start()
                else:
                    out_rows[z] = z_out[h, i * capacity : (i + 1) * capacity, :]

        for h in range(2):
            multiply(h, 0)
            send_mate(h, 0)
            if h == 1:
                finish(0)
            multiply(h, 1)
            m_copies[h, 0].wait_recv()
            x_out[h] = (part[h, 0] + m_land[h, 0].astype(jnp.float32)).astype(jnp.bfloat16)
            x_copies[h] = remote(
                x_out.at[h], x_land.at[h], x_send.at[h], x_recv.at[h], over_x
            )
            x_copies[h].start()
            if h == 0:
                s_m.wait_recv()
                s_x[...] = scal_ref[...] + s_land[...]
                s_xc = remote(s_x, s_xland, sx_send, sx_recv, over_x)
                s_xc.start()
            multiply(h, 2)
            send_mate(h, 1)
            if h == 0:
                s_xc.wait_recv()
                s_z[...] = s_x[...] + s_xland[...]
                for j in range(1, experts):
                    copy = remote(
                        s_z.at[zs[j]], out_scal.at[z], sz_send.at[j], sz_recv.at[j],
                        {"expert": zs[j]},
                    )
                    copy.start()
                    s_copies.append(copy)
                out_scal[z] = s_z[z]
            multiply(h, 3)
        finish(1)
        for copy in list(z_copies.values()) + s_copies:
            copy.wait_recv()
        for copy in list(m_copies.values()) + list(x_copies.values()) + [s_m, s_xc]:
            copy.wait_send()
        for copy in list(z_copies.values()) + s_copies:
            copy.wait_send()

    f32, bf16, dma = jnp.float32, jnp.bfloat16, pltpu.SemaphoreType.DMA
    vmem = pl.BlockSpec(memory_space=pltpu.VMEM)
    anywhere = pl.BlockSpec(memory_space=pl.ANY)
    return pl.pallas_call(
        kernel,
        out_shape=(
            jax.ShapeDtypeStruct((experts, capacity, cols), bf16),
            jax.ShapeDtypeStruct(scalars.shape, f32),
        ),
        in_specs=[vmem, vmem, anywhere, anywhere, vmem],
        out_specs=[vmem] * 2,
        scratch_shapes=[
            pltpu.VMEM((2, 2 * half, width), bf16),
            pltpu.VMEM((2, 4, cols, width), bf16),
            pltpu.VMEM((2, 2, half, cols), f32),
            pltpu.VMEM((2, 2, half, cols), bf16),
            pltpu.VMEM((2, 2, half, cols), bf16),
            pltpu.VMEM((2, half, cols), bf16),
            pltpu.VMEM((2, half, cols), bf16),
            pltpu.VMEM((2, half, cols), bf16),
            pltpu.VMEM(scalars.shape, f32),
            pltpu.VMEM(scalars.shape, f32),
            pltpu.VMEM(scalars.shape, f32),
            pltpu.VMEM(scalars.shape, f32),
            dma((2, 4)),
            dma((2, 2)), dma((2, 2)),
            dma((2,)), dma((2,)),
            dma((experts,)), dma((experts,)),
            dma, dma, dma, dma,
            dma((experts,)), dma((experts,)),
        ],
        compiler_params=pltpu.CompilerParams(
            collective_id=3, has_side_effects=True, vmem_limit_bytes=58 * 1024 * 1024
        ),
    )(gate_grad, up_grad, gate_matrix, up_matrix, scalars)


def body(
    hidden_in, norm_gain, router_weight, routes, gate_weight, up_weight, down_weight, grad_out
):
    tok_rows, part_cols = hidden_in.shape
    expert_count = router_weight.shape[1]
    feat_width = part_cols * lax.axis_size("tensor")
    capacity = 8 * tok_rows // (3 * expert_count)
    direct = lax.axis_size("tensor") == 4 and expert_count == 4 and part_cols % STRIP == 0 and down_weight.shape[1] % STRIP == 0
    inputs_f = hidden_in.astype(jnp.float32)
    scaled_in = inputs_f * norm_gain[None, :]
    square_part = jnp.sum(inputs_f * inputs_f, axis=1)
    logit_part = jnp.einsum("td,de->et", scaled_in, router_weight, precision=PRECISE)
    token_part = jnp.concatenate([square_part[None, :], logit_part], axis=0)
    if direct:
        padding = ((0, -token_part.shape[0] % 8), (0, -tok_rows % 128))
        token_sum = small_psum(jnp.pad(token_part, padding), "tensor", 0)
    else:
        token_sum = lax.psum(token_part, "tensor")
    square_sum = token_sum[0, :tok_rows]
    logit_sum = token_sum[1 : 1 + expert_count, :tok_rows].T
    inv_rms = lax.rsqrt(square_sum / feat_width + EPS)[:, None]
    normed = scaled_in * inv_rms
    normed_b = normed.astype(jnp.bfloat16)
    logits = logit_sum * inv_rms
    labels = jnp.arange(expert_count, dtype=jnp.int32)
    first_hot = (routes[:, 0:1] == labels[None, :]).astype(jnp.float32)
    second_hot = (routes[:, 1:2] == labels[None, :]).astype(jnp.float32)
    prob_first = jax.nn.sigmoid(jnp.sum(logits * (first_hot - second_hot), axis=1))
    prob_second = 1.0 - prob_first
    flat_routes = routes.reshape(-1)
    route_hot = (flat_routes[:, None] == labels[None, :]).astype(jnp.int32)
    slot_rank = jnp.sum(
        (jnp.cumsum(route_hot, axis=0, dtype=jnp.int32) - route_hot) * route_hot,
        axis=1,
        dtype=jnp.int32,
    )
    slot_index = (flat_routes * capacity + slot_rank).reshape(tok_rows, 2)
    slot_ids = jnp.arange(expert_count * capacity, dtype=jnp.int32)
    pick_first = (slot_index[:, 0:1] == slot_ids[None, :]).astype(jnp.float32)
    pick_second = (slot_index[:, 1:2] == slot_ids[None, :]).astype(jnp.float32)
    pick_both = pick_first + pick_second
    pick_bf = pick_both.astype(jnp.bfloat16)
    prob_first_b = prob_first.astype(jnp.bfloat16)
    prob_second_b = prob_second.astype(jnp.bfloat16)
    pick_weight = (
        pick_first * prob_first_b.astype(jnp.float32)[:, None]
        + pick_second * prob_second_b.astype(jnp.float32)[:, None]
    ).astype(jnp.bfloat16)

    def dispatch(pick, row_block):
        placed = jnp.einsum("ts,td->sd", pick, row_block, preferred_element_type=jnp.float32)
        return placed.astype(jnp.bfloat16).reshape(expert_count, capacity, row_block.shape[1])

    send_grads = dispatch(pick_weight, grad_out)
    send_rows = dispatch(pick_bf, normed_b)
    slot_total = expert_count * capacity
    if direct:
        out_grad, slot_rows, act_grad, gate_pre = gather_slots(
            send_grads, send_rows, down_weight[0], gate_weight[0]
        )
    else:
        got_rows = lax.all_to_all(send_rows, "expert", split_axis=0, concat_axis=0, tiled=True)
        got_grads = lax.all_to_all(send_grads, "expert", split_axis=0, concat_axis=0, tiled=True)
        slot_rows = lax.all_gather(got_rows, "tensor", axis=2, tiled=True)
        slot_rows = slot_rows.reshape(slot_total, feat_width)
        out_grad = lax.all_gather(got_grads, "tensor", axis=2, tiled=True)
        out_grad = out_grad.reshape(slot_total, feat_width)
    gate_matrix = gate_weight[0]
    up_matrix = up_weight[0]
    down_matrix = down_weight[0]
    if not direct:
        gate_pre = jnp.dot(slot_rows, gate_matrix, preferred_element_type=jnp.float32)
    up_pre = jnp.dot(slot_rows, up_matrix, preferred_element_type=jnp.float32)
    gate_sig = jax.nn.sigmoid(gate_pre)
    hidden_act = (gate_pre * gate_sig * up_pre).astype(jnp.bfloat16)
    grad_down = jnp.einsum(
        "sf,sd->fd", hidden_act, out_grad, preferred_element_type=jnp.float32
    ).astype(jnp.bfloat16)[None]
    if not direct:
        act_grad = jnp.einsum("sd,fd->sf", out_grad, down_matrix, preferred_element_type=jnp.float32)
    gate_grad = (act_grad * up_pre * gate_sig * (1.0 + gate_pre * (1.0 - gate_sig))).astype(
        jnp.bfloat16
    )
    up_grad = (act_grad * gate_pre * gate_sig).astype(jnp.bfloat16)
    prob_part = jnp.sum(hidden_act.astype(jnp.float32) * act_grad, axis=1)
    inner_part = jnp.sum(
        gate_grad.astype(jnp.float32) * gate_pre + up_grad.astype(jnp.float32) * up_pre, axis=1
    )
    if direct:
        scalars = jnp.stack([inner_part, prob_part], axis=0).reshape(2, expert_count, capacity)
        scalars = jnp.pad(scalars.transpose(1, 0, 2), ((0, 0), (0, 6), (0, 0)))
        back_rows, scalars = return_slots(
            gate_grad, up_grad, gate_matrix, up_matrix, scalars, expert_count, capacity, part_cols
        )
        back_rows = back_rows.reshape(slot_total, part_cols)
        scalars = scalars[:, :2].transpose(1, 0, 2).reshape(2, slot_total)
    else:
        row_part = jnp.einsum("sf,df->sd", gate_grad, gate_matrix, preferred_element_type=jnp.float32)
        row_part = row_part + jnp.einsum(
            "sf,df->sd", up_grad, up_matrix, preferred_element_type=jnp.float32
        )
        row_part = row_part.astype(jnp.bfloat16)
        row_own = lax.psum_scatter(
            row_part, "tensor", scatter_dimension=1, tiled=True
        )
        back_rows = lax.all_to_all(
            row_own.reshape(-1, capacity, part_cols), "expert", split_axis=0, concat_axis=0, tiled=True
        ).reshape(expert_count * capacity, part_cols)
        scalars = jnp.stack([inner_part, prob_part], axis=0).reshape(2, -1, capacity)
        scalars = lax.all_to_all(scalars, "expert", split_axis=1, concat_axis=1, tiled=True)
        scalars = scalars.reshape(2, expert_count * capacity)
    pick_token = jnp.concatenate([pick_first, pick_second], axis=0)
    token_scalars = jnp.einsum("cs,ts->ct", scalars, pick_token, precision=PRECISE)
    if not direct:
        token_scalars = lax.psum(token_scalars, "tensor")
    token_scalars = token_scalars.reshape(2, 2, tok_rows)
    expert_grad = jnp.dot(pick_bf, back_rows, preferred_element_type=jnp.float32)
    token_inner = token_scalars[0, 0] + token_scalars[0, 1]
    ratio_first = prob_first / jnp.where(prob_first_b == 0, 1, prob_first_b).astype(jnp.float32)
    ratio_second = prob_second / jnp.where(prob_second_b == 0, 1, prob_second_b).astype(jnp.float32)
    gap_grad = (
        token_scalars[1, 0] * ratio_first * prob_second
        - token_scalars[1, 1] * ratio_second * prob_first
    )
    logit_grad = gap_grad[:, None] * (first_hot - second_hot)
    total_grad = expert_grad + jnp.einsum("te,de->td", logit_grad, router_weight, precision=PRECISE)
    norm_dot = (token_inner + jnp.sum(logits * logit_grad, axis=1)) / inv_rms[:, 0]
    cubed = inv_rms * inv_rms * inv_rms
    grad_input = (
        inv_rms * norm_gain[None, :] * total_grad
        - inputs_f * cubed * (norm_dot[:, None] / feat_width)
    ).astype(jnp.bfloat16)
    gain_part = jnp.sum(total_grad * inputs_f * inv_rms, axis=0)
    router_part = jnp.einsum("td,te->de", normed, logit_grad, precision=PRECISE)
    sums = jnp.concatenate([gain_part[None, :], router_part.T], axis=0)
    if direct:
        sums = small_psum(jnp.pad(sums, ((0, -sums.shape[0] % 8), (0, 0))), "expert", 1)
        sums = sums[: 1 + expert_count]
    else:
        sums = lax.psum(sums, "expert")
    grad_gain, grad_router = sums[0], sums[1:].T
    return (grad_input, grad_gain, grad_router, grad_down)


def solution(mesh):
    placed = (
        P(("groups", "expert"), "tensor"),
        P("tensor"),
        P("tensor", None),
        P(("groups", "expert"), None),
        P("expert", None, "tensor"),
        P("expert", None, "tensor"),
        P("expert", "tensor", None),
        P(("groups", "expert"), "tensor"),
    )
    return jax.shard_map(
        body,
        mesh=mesh,
        in_specs=placed,
        out_specs=(
            P(("groups", "expert"), "tensor"),
            P(("groups", "tensor")),
            P(("groups", "tensor"), None),
            P(("groups", "expert"), "tensor", None),
        ),
        check_vma=False,
    )
```
